32 devices in a mesh: grp: 2 (over x), own: 16 (over z, y, core).
Axes of the slice: x: 2, y: 2, z: 4, core: 2. Of those that a mesh axis runs over, the one named last changes fastest.
Arguments:
- left: bfloat16 [2048, 128, 64], P(('grp', 'own')), may hold values from -0.75 to 0.75
- right: bfloat16 [2048, 128, 64], P(('grp', 'own')), may hold values from -0.75 to 0.75
- values: bfloat16 [2048, 128], P(('grp', 'own')), may hold values from -6 to 6
- core: bfloat16 [10240, 64, 64], P(('grp', 'own')), may hold values from -6 to 6
- tile_slice: int32 [2048], P(('grp', 'own')), may hold values from 0 to 10239, as said below
- tile_fill: int32 [2048], P(('grp', 'own')), may hold values from 64 to 128
Outputs:
- new_core: bfloat16 [10240, 64, 64], P(('grp', 'own'))
- new_left: bfloat16 [2048, 128, 64], P(('grp', 'own'))
The draws below stay inside these ranges and needn't reach their ends.
Inputs may be any that keep to these rules, and one draw needn't show every extreme that they name: `tile_slice`: call j // 320 the block of slice j and its remainder mod 16 its class. Among the tiles of one device at most 8 have slices of one class; in every group of 16 consecutive devices some class gets exactly 8 tiles from every device of the group.
All inputs are finite; a program needn't handle non-finite values.
Results may differ from the reference program's by a relative error of at most 0.0052.
Values may be sent and summed in bfloat16 or wider, within the bound.
A program may use at most 128 MiB of HBM per device.

```python
import jax
import jax.numpy as jnp
from jax import lax

RANK = 64
TILE = 128
SLICES = 10240
TILES_DEV = 64
TILES = 2048
OWNERS = 16
GROUPS = 2
SL_DEV = 320


def draw_tile_slice(key, part):
    dev_total = TILES // TILES_DEV
    fill_base = TILES_DEV // OWNERS
    slot_cap = 2 * fill_base
    pair_count = OWNERS // 2

    def one_device(device):
        key_block = jax.random.fold_in(key, device)
        key_group = jax.random.fold_in(jax.random.fold_in(key, 7919), device // OWNERS)
        shifts = jax.random.randint(jax.random.fold_in(key_block, 1), (pair_count,), -fill_base, fill_base + 1)
        chosen = jax.random.randint(key_group, (), 0, pair_count)
        sign_value = 2 * jax.random.randint(jax.random.fold_in(key_group, 1), (), 0, 2) - 1
        shifts = jnp.where(jnp.arange(pair_count) == chosen, sign_value * fill_base, shifts)
        counts = jnp.stack([fill_base + shifts, fill_base - shifts], axis=1).reshape(-1)
        slot_owner = jnp.repeat(jnp.arange(OWNERS), slot_cap)
        slot_rank = jnp.tile(jnp.arange(slot_cap), OWNERS)
        live_slots = slot_rank < counts[slot_owner]
        slot_order = jnp.argsort(jnp.where(live_slots, 0, 1), stable=True)
        chosen_owner = slot_owner[slot_order[:TILES_DEV]]
        chosen_owner = jax.random.permutation(jax.random.fold_in(key_block, 2), chosen_owner)
        group_pick = jax.random.randint(jax.random.fold_in(key_block, 3), (TILES_DEV,), 0, GROUPS)
        offsets = jax.random.randint(jax.random.fold_in(key_block, 4), (TILES_DEV,), 0, SL_DEV)
        return ((group_pick * OWNERS + chosen_owner) * SL_DEV + offsets).astype(jnp.int32)
    return jax.vmap(one_device)(jnp.arange(dev_total)).reshape(-1)


def place_ends(values, stream_key, smallest, high):
    longest = values.shape.index(max(values.shape))
    spots = []
    for shift in (0, 1):
        where = [jax.random.randint(jax.random.fold_in(stream_key, axis), (), 0, length) for axis, length in enumerate(values.shape)]
        where[longest] = (where[longest] + shift) % values.shape[longest]
        spots.append(tuple(where))
    return values.at[spots[0]].set(smallest).at[spots[1]].set(high)


def level_of(key, extent, split, smallest, top_value):
    loudness, own = 1.0, jax.random.fold_in(key, 6)
    for position, parts in split:
        steps = jnp.exp(jax.random.uniform(jax.random.fold_in(own, position), (parts,), jnp.float32, smallest / len(split), top_value / len(split)))
        loudness = loudness * jnp.repeat(steps, extent[position] // parts).reshape([-1 if axis == position else 1 for axis in range(len(extent))])
    return loudness


def normal_values(stream_key, shape, spread, reach, shards=(), kind=jnp.bfloat16):
    gain = level_of(stream_key, shape, shards, -0.22, 0.18) if shards else 1.0
    entries = jax.random.normal(stream_key, shape, jnp.float32) * spread * gain
    return jnp.minimum(jnp.maximum(entries, -reach), reach).astype(kind)


def setup_inputs(seed: int = 0) -> dict:
    keys = jax.random.split(jax.random.key(seed), 7)
    left = normal_values(keys[0], (TILES, TILE, RANK), 0.125, 0.75, ((0, 32),))
    right = normal_values(keys[1], (TILES, TILE, RANK), 0.125, 0.75, ((0, 32),))
    values = normal_values(keys[2], (TILES, TILE), 1.0, 6.0, ((0, 32),))
    core = normal_values(keys[3], (SLICES, RANK, RANK), 1.0, 6.0, ((0, 32),))
    tile_slice = draw_tile_slice(jax.random.fold_in(keys[6], 71), 0)
    tile_fill = place_ends(jax.random.randint(keys[5], (TILES,), TILE // 2, TILE + 1), jax.random.fold_in(keys[5], 1), TILE // 2, TILE).astype(jnp.int32)
    return dict(left=left, right=right, values=values, core=core, tile_slice=tile_slice, tile_fill=tile_fill)


def tile_gradients(packed):
    left_tiles, right_tiles, value_tiles, slice_ids, fill_counts, core_table = packed
    slice_tables = core_table[slice_ids].astype(jnp.float32)
    projected = jnp.einsum('sea,sab->seb', left_tiles.astype(jnp.float32), slice_tables, precision=lax.Precision.HIGHEST)
    predicted = jnp.sum(projected * right_tiles.astype(jnp.float32), axis=-1)
    live_rows = jnp.arange(TILE)[None, :] < fill_counts[:, None]
    residual = jnp.where(live_rows, predicted - value_tiles.astype(jnp.float32), jnp.float32(0.0))
    weighted = (residual[:, :, None] * left_tiles.astype(jnp.float32)).astype(jnp.bfloat16)
    return jnp.einsum('sea,seb->sab', weighted.astype(jnp.float32), right_tiles.astype(jnp.float32), precision=lax.Precision.HIGHEST)


def reference(left, right, values, core, tile_slice, tile_fill):
    block_count = TILES // TILES_DEV
    left_blocks = left.reshape(block_count, TILES_DEV, TILE, RANK)
    right_blocks = right.reshape(block_count, TILES_DEV, TILE, RANK)
    value_blocks = values.reshape(block_count, TILES_DEV, TILE)
    slice_blocks = tile_slice.reshape(block_count, TILES_DEV)
    fill_blocks = tile_fill.reshape(block_count, TILES_DEV)

    def grads_of(index):
        return tile_gradients((left_blocks[index], right_blocks[index], value_blocks[index], slice_blocks[index], fill_blocks[index], core))

    tile_grads = lax.map(grads_of, jnp.arange(block_count)).reshape(TILES, RANK, RANK)
    gradient = jax.ops.segment_sum(tile_grads, tile_slice, num_segments=SLICES)
    new_core = (core.astype(jnp.float32) - gradient).astype(jnp.bfloat16)

    def refresh_of(index):
        slice_tables = new_core[slice_blocks[index]].astype(jnp.float32)
        refreshed = jnp.einsum('sea,sab->seb', left_blocks[index].astype(jnp.float32), slice_tables, precision=lax.Precision.HIGHEST)
        return refreshed.astype(jnp.bfloat16)

    new_left = lax.map(refresh_of, jnp.arange(block_count)).reshape(TILES, TILE, RANK)
    return new_core, new_left
```

```python
import jax
import jax.numpy as jnp
from jax import lax
from jax.sharding import PartitionSpec as P


def pack(x):
    half = x.shape[-2] // 2
    return jnp.concatenate([x[..., :half, :], x[..., half:, :]], axis=-1)


def unpack(x):
    half = x.shape[-1] // 2
    return jnp.concatenate([x[..., :half], x[..., half:]], axis=-2)


def body(left, right, values, core, tile_slice, tile_fill):
    owners = lax.axis_size("own")
    groups = lax.axis_size("grp")
    tile_count, tile_rows, rank = left.shape
    per_device = core.shape[0]
    cap = 2 * tile_count // owners
    slots = owners * cap
    grp = lax.axis_index("grp")
    block = tile_slice // per_device
    owner = block % owners
    place = block // owners * per_device + tile_slice % per_device
    pos = jnp.arange(tile_count)
    earlier = (owner[:, None] == owner[None, :]) & (pos[None, :] < pos[:, None])
    slot_of_tile = owner * cap + jnp.sum(earlier.astype(jnp.int32), axis=1)
    match = slot_of_tile[None, :] == jnp.arange(slots)[:, None]
    live = jnp.any(match, axis=1)
    tile_of_slot = jnp.sum(jnp.where(match, pos[None, :], 0), axis=1)
    want = jnp.sum(jnp.where(match, place[None, :] + 1, 0), axis=1) - 1
    table = lax.all_to_all(
        jnp.broadcast_to(want.reshape(1, owners, cap), (groups, owners, cap)).reshape(groups * owners, cap),
        ("grp", "own"), split_axis=0, concat_axis=0, tiled=True,
    ).reshape(groups, slots)

    def shifted(step):
        return (grp + step) % groups

    local = jnp.clip(table - grp * per_device, 0, per_device - 1)
    packed = pack(core)
    mine = table[grp]
    old = packed[local[grp]]
    for step in range(1, groups):
        perm = [(g, (g + step) % groups) for g in range(groups)]
        got = lax.ppermute(packed[local[shifted(step)]], "grp", perm)
        old = jnp.where((mine // per_device == shifted(-step))[:, None, None], got, old)
    slices = lax.all_to_all(old, "own", split_axis=0, concat_axis=0, tiled=True)
    tables = unpack(slices[slot_of_tile])

    projected = jnp.einsum("sea,sab->seb", left, tables, preferred_element_type=jnp.float32)
    predicted = jnp.sum(projected * right.astype(jnp.float32), axis=-1)
    live_rows = jnp.arange(tile_rows)[None, :] < tile_fill[:, None]
    residual = jnp.where(live_rows, predicted - values.astype(jnp.float32), 0.0)
    weighted = (residual[:, :, None] * left.astype(jnp.float32)).astype(jnp.bfloat16)
    grad = jnp.einsum("sea,seb->sab", weighted, right, preferred_element_type=jnp.float32).astype(jnp.bfloat16)
    send = jnp.where(live[:, None, None], pack(grad)[tile_of_slot], jnp.bfloat16(0))
    grads = lax.all_to_all(send, "own", split_axis=0, concat_axis=0, tiled=True)
    parts, places = [grads], [mine]
    for step in range(1, groups):
        perm = [(g, (g + step) % groups) for g in range(groups)]
        parts.append(lax.ppermute(grads, "grp", perm))
        places.append(table[shifted(-step)])
    flat = jnp.concatenate(parts, axis=0)
    place_of = jnp.concatenate(places, axis=0)
    pick = (mine[:, None] == place_of[None, :]).astype(jnp.bfloat16)
    total = jnp.einsum("st,tab->sab", pick, flat, preferred_element_type=jnp.float32)
    fresh = (old.astype(jnp.float32) - total).astype(jnp.bfloat16)
    back = lax.all_to_all(fresh, "own", split_axis=0, concat_axis=0, tiled=True)
    ids = grp * per_device + jnp.arange(per_device)
    pick_core = (ids[:, None] == place_of[None, :]).astype(jnp.bfloat16)
    total_core = jnp.einsum("st,tab->sab", pick_core, flat, preferred_element_type=jnp.float32)
    new_core = (core.astype(jnp.float32) - unpack(total_core)).astype(jnp.bfloat16)
    new_left = jnp.einsum(
        "sea,sab->seb", left, unpack(back[slot_of_tile]), preferred_element_type=jnp.float32
    ).astype(jnp.bfloat16)
    return new_core, new_left


def solution(mesh):
    tiles = P(("grp", "own"), None, None)
    return jax.shard_map(
        body,
        mesh=mesh,
        in_specs=(tiles, tiles, P(("grp", "own"), None), tiles, P(("grp", "own")), P(("grp", "own"))),
        out_specs=(tiles, tiles),
        check_vma=False,
    )
```

```python
import jax
import jax.numpy as jnp
from jax import lax
from jax.experimental import pallas as pl
from jax.experimental.pallas import tpu as pltpu
from jax.sharding import PartitionSpec as P


def pack(x):
    half = x.shape[-2] // 2
    return jnp.concatenate([x[..., :half, :], x[..., half:, :]], axis=-1)


def unpack(x):
    half = x.shape[-1] // 2
    return jnp.concatenate([x[..., :half], x[..., half:]], axis=-2)


CHUNKS = 1


def one_hot(places, width):
    lanes = lax.broadcasted_iota(jnp.int32, (places.shape[0], width), 1)
    return (places == lanes).astype(jnp.float32).astype(jnp.bfloat16)


def fetch_kernel(place_ref, core_ref, out_ref):
    half = out_ref.shape[0]
    hot = one_hot(place_ref[...], core_ref.shape[2])

    def step(i, carry):
        slab = jnp.concatenate([core_ref[i], core_ref[i + half]], axis=0)
        out_ref[i] = lax.dot_general(
            hot, slab, (((1,), (1,)), ((), ())), preferred_element_type=jnp.float32
        ).astype(out_ref.dtype)
        return carry

    lax.fori_loop(0, half, step, 0, unroll=2)


def fetch(core_t, places):
    rank, _, count = core_t.shape
    wanted = places.shape[0]
    return pl.pallas_call(
        fetch_kernel,
        out_shape=jax.ShapeDtypeStruct((rank // 2, wanted, 2 * rank), core_t.dtype),
        compiler_params=pltpu.CompilerParams(vmem_limit_bytes=48 * 2**20),
        cost_estimate=pl.CostEstimate(
            flops=2 * wanted * count * rank * rank, bytes_accessed=2 * rank * rank * (count + wanted), transcendentals=0
        ),
    )(places, core_t)


def apply_kernel(place_ref, core_ref, grads_ref, out_ref):
    half = grads_ref.shape[0]
    rank = out_ref.shape[1]
    hot = one_hot(place_ref[...], core_ref.shape[2])

    def step(i, carry):
        total = lax.dot_general(
            grads_ref[i], hot, (((0,), (0,)), ((), ())), preferred_element_type=jnp.float32
        )
        for part, row in ((0, i), (1, i + half)):
            change = total[part * rank:(part + 1) * rank]
            out_ref[row] = (core_ref[row].astype(jnp.float32) - change).astype(out_ref.dtype)
        return carry

    lax.fori_loop(0, half, step, 0, unroll=2)


def apply_grads(core_t, grads, places):
    rank, _, count = core_t.shape
    wanted = places.shape[0]
    return pl.pallas_call(
        apply_kernel,
        out_shape=jax.ShapeDtypeStruct(core_t.shape, core_t.dtype),
        compiler_params=pltpu.CompilerParams(vmem_limit_bytes=48 * 2**20),
        cost_estimate=pl.CostEstimate(
            flops=2 * wanted * count * rank * rank,
            bytes_accessed=2 * rank * rank * (2 * count + wanted),
            transcendentals=0,
        ),
    )(places, core_t, grads)


def body(left, right, values, core, tile_slice, tile_fill):
    owners = lax.axis_size("own")
    groups = lax.axis_size("grp")
    tile_count, tile_rows, rank = left.shape
    per_device = core.shape[0]
    cap = 2 * tile_count // owners
    slots = owners * cap
    grp = lax.axis_index("grp")
    block = tile_slice // per_device
    owner = block % owners
    place = block // owners * per_device + tile_slice % per_device
    pos = jnp.arange(tile_count)
    earlier = (owner[:, None] == owner[None, :]) & (pos[None, :] < pos[:, None])
    slot_of_tile = owner * cap + jnp.sum(earlier.astype(jnp.int32), axis=1)
    match = slot_of_tile[None, :] == jnp.arange(slots)[:, None]
    live = jnp.any(match, axis=1)
    tile_of_slot = jnp.sum(jnp.where(match, pos[None, :], 0), axis=1)
    want = jnp.sum(jnp.where(match, place[None, :] + 1, 0), axis=1) - 1
    table = lax.all_to_all(
        jnp.broadcast_to(want.reshape(1, owners, cap), (groups, owners, cap)).reshape(groups * owners, cap),
        ("grp", "own"), split_axis=0, concat_axis=0, tiled=True,
    ).reshape(groups, slots)

    def shifted(step):
        return (grp + step) % groups

    core_t = jnp.transpose(core, (1, 2, 0))
    local = table - grp * per_device
    mine = table[grp]
    order = [shifted(step) for step in range(groups)]
    found = fetch(core_t, jnp.concatenate([local[g] for g in order])[:, None])
    half = found.shape[0] // CHUNKS
    olds, slices = [], []
    for c in range(CHUNKS):
        rows = jnp.transpose(found[c * half:(c + 1) * half], (1, 0, 2))
        old = rows[:slots]
        for step in range(1, groups):
            perm = [(g, (g + step) % groups) for g in range(groups)]
            got = lax.ppermute(rows[step * slots:(step + 1) * slots], "grp", perm)
            old = old + got
        olds.append(old)
        slices.append(lax.all_to_all(old, "own", split_axis=0, concat_axis=0, tiled=True))
    old = jnp.concatenate(olds, axis=1)
    slices = jnp.concatenate(slices, axis=1)
    tables = unpack(slices[slot_of_tile])

    projected = jnp.einsum("sea,sab->seb", left, tables, preferred_element_type=jnp.float32)
    predicted = jnp.sum(projected * right.astype(jnp.float32), axis=-1)
    live_rows = jnp.arange(tile_rows)[None, :] < tile_fill[:, None]
    residual = jnp.where(live_rows, predicted - values.astype(jnp.float32), 0.0)
    weighted = (residual[:, :, None] * left.astype(jnp.float32)).astype(jnp.bfloat16)
    grad = jnp.einsum("sea,seb->sab", weighted, right, preferred_element_type=jnp.float32).astype(jnp.bfloat16)
    send = jnp.where(live[:, None, None], pack(grad)[tile_of_slot], jnp.bfloat16(0))
    pieces, places = [], [mine]
    for c in range(CHUNKS):
        grads = lax.all_to_all(
            send[:, c * half:(c + 1) * half], "own", split_axis=0, concat_axis=0, tiled=True
        )
        parts = [grads]
        for step in range(1, groups):
            perm = [(g, (g + step) % groups) for g in range(groups)]
            parts.append(lax.ppermute(grads, "grp", perm))
        pieces.append(jnp.concatenate(parts, axis=0))
    for step in range(1, groups):
        places.append(table[shifted(-step)])
    flat = jnp.concatenate(pieces, axis=1)
    place_of = jnp.concatenate(places, axis=0)
    pick = (mine[:, None] == place_of[None, :]).astype(jnp.bfloat16)
    total = jnp.einsum("st,tab->sab", pick, flat, preferred_element_type=jnp.float32)
    fresh = (old.astype(jnp.float32) - total).astype(jnp.bfloat16)
    back = lax.all_to_all(fresh, "own", split_axis=0, concat_axis=0, tiled=True)
    new_core_t = apply_grads(core_t, jnp.transpose(flat, (1, 0, 2)), (place_of - grp * per_device)[:, None])
    new_core = jnp.transpose(new_core_t, (2, 0, 1))
    new_left = jnp.einsum(
        "sea,sab->seb", left, unpack(back[slot_of_tile]), preferred_element_type=jnp.float32
    ).astype(jnp.bfloat16)
    return new_core, new_left


def solution(mesh):
    tiles = P(("grp", "own"), None, None)
    return jax.shard_map(
        body,
        mesh=mesh,
        in_specs=(tiles, tiles, P(("grp", "own"), None), tiles, P(("grp", "own")), P(("grp", "own"))),
        out_specs=(tiles, tiles),
        check_vma=False,
    )
```

```python
import jax
import jax.numpy as jnp
from jax import lax
from jax.experimental import pallas as pl
from jax.experimental.pallas import tpu as pltpu
from jax.sharding import PartitionSpec as P


def pack(x):
    half = x.shape[-2] // 2
    return jnp.concatenate([x[..., :half, :], x[..., half:, :]], axis=-1)


def unpack(x):
    half = x.shape[-1] // 2
    return jnp.concatenate([x[..., :half], x[..., half:]], axis=-2)


CHUNKS = 2


def one_hot(places, width):
    lanes = lax.broadcasted_iota(jnp.int32, (places.shape[0], width), 1)
    return (places == lanes).astype(jnp.float32).astype(jnp.bfloat16)


def fetch_kernel(place_ref, core_ref, out_ref):
    half = out_ref.shape[0]
    hot = one_hot(place_ref[...], core_ref.shape[2])

    def step(i, carry):
        slab = jnp.concatenate([core_ref[i], core_ref[i + half]], axis=0)
        out_ref[i] = lax.dot_general(
            hot, slab, (((1,), (1,)), ((), ())), preferred_element_type=jnp.float32
        ).astype(out_ref.dtype)
        return carry

    lax.fori_loop(0, half, step, 0, unroll=2)


def fetch(core_t, places):
    rank, _, count = core_t.shape
    wanted = places.shape[0]
    return pl.pallas_call(
        fetch_kernel,
        out_shape=jax.ShapeDtypeStruct((rank // 2, wanted, 2 * rank), core_t.dtype),
        compiler_params=pltpu.CompilerParams(vmem_limit_bytes=48 * 2**20),
        cost_estimate=pl.CostEstimate(
            flops=2 * wanted * count * rank * rank, bytes_accessed=2 * rank * rank * (count + wanted), transcendentals=0
        ),
    )(places, core_t)


def apply_kernel(place_ref, core_ref, grads_ref, out_ref):
    half = grads_ref.shape[0]
    rank = out_ref.shape[1]
    hot = one_hot(place_ref[...], core_ref.shape[2])

    def step(i, carry):
        total = lax.dot_general(
            grads_ref[i], hot, (((0,), (0,)), ((), ())), preferred_element_type=jnp.float32
        )
        for part, row in ((0, i), (1, i + half)):
            change = total[part * rank:(part + 1) * rank]
            out_ref[row] = (core_ref[row].astype(jnp.float32) - change).astype(out_ref.dtype)
        return carry

    lax.fori_loop(0, half, step, 0, unroll=2)


def apply_grads(core_t, grads, places):
    rank, _, count = core_t.shape
    wanted = places.shape[0]
    return pl.pallas_call(
        apply_kernel,
        out_shape=jax.ShapeDtypeStruct(core_t.shape, core_t.dtype),
        compiler_params=pltpu.CompilerParams(vmem_limit_bytes=48 * 2**20),
        cost_estimate=pl.CostEstimate(
            flops=2 * wanted * count * rank * rank,
            bytes_accessed=2 * rank * rank * (2 * count + wanted),
            transcendentals=0,
        ),
    )(places, core_t, grads)


def body(left, right, values, core, tile_slice, tile_fill):
    owners = lax.axis_size("own")
    groups = lax.axis_size("grp")
    tile_count, tile_rows, rank = left.shape
    per_device = core.shape[0]
    cap = 2 * tile_count // owners
    slots = owners * cap
    grp = lax.axis_index("grp")
    block = tile_slice // per_device
    owner = block % owners
    place = block // owners * per_device + tile_slice % per_device
    pos = jnp.arange(tile_count)
    earlier = (owner[:, None] == owner[None, :]) & (pos[None, :] < pos[:, None])
    slot_of_tile = owner * cap + jnp.sum(earlier.astype(jnp.int32), axis=1)
    match = slot_of_tile[None, :] == jnp.arange(slots)[:, None]
    live = jnp.any(match, axis=1)
    tile_of_slot = jnp.sum(jnp.where(match, pos[None, :], 0), axis=1)
    want = jnp.sum(jnp.where(match, place[None, :] + 1, 0), axis=1) - 1
    table = lax.all_to_all(
        jnp.broadcast_to(want.reshape(1, owners, cap), (groups, owners, cap)).reshape(groups * owners, cap),
        ("grp", "own"), split_axis=0, concat_axis=0, tiled=True,
    ).reshape(groups, slots)

    def shifted(step):
        return (grp + step) % groups

    core_t = jnp.transpose(core, (1, 2, 0))
    local = table - grp * per_device
    mine = table[grp]
    order = [shifted(step) for step in range(groups)]
    found = fetch(core_t, jnp.concatenate([local[g] for g in order])[:, None])
    half = found.shape[0] // CHUNKS
    olds, slices = [], []
    for c in range(CHUNKS):
        rows = jnp.transpose(found[c * half:(c + 1) * half], (1, 0, 2))
        old = rows[:slots]
        for step in range(1, groups):
            perm = [(g, (g + step) % groups) for g in range(groups)]
            got = lax.ppermute(rows[step * slots:(step + 1) * slots], "grp", perm)
            old = old + got
        olds.append(old)
        slices.append(lax.all_to_all(old, "own", split_axis=0, concat_axis=0, tiled=True))
    old = jnp.concatenate(olds, axis=1)
    slices = jnp.concatenate(slices, axis=1)
    tables = unpack(slices[slot_of_tile])

    projected = jnp.einsum("sea,sab->seb", left, tables, preferred_element_type=jnp.float32)
    predicted = jnp.sum(projected * right.astype(jnp.float32), axis=-1)
    live_rows = jnp.arange(tile_rows)[None, :] < tile_fill[:, None]
    residual = jnp.where(live_rows, predicted - values.astype(jnp.float32), 0.0)
    weighted = (residual[:, :, None] * left.astype(jnp.float32)).astype(jnp.bfloat16)
    grad = jnp.einsum("sea,seb->sab", weighted, right, preferred_element_type=jnp.float32).astype(jnp.bfloat16)
    send = jnp.where(live[:, None, None], pack(grad)[tile_of_slot], jnp.bfloat16(0))
    pieces, places = [], [mine]
    for c in range(CHUNKS):
        grads = lax.all_to_all(
            send[:, c * half:(c + 1) * half], "own", split_axis=0, concat_axis=0, tiled=True
        )
        parts = [grads]
        for step in range(1, groups):
            perm = [(g, (g + step) % groups) for g in range(groups)]
            parts.append(lax.ppermute(grads, "grp", perm))
        pieces.append(jnp.concatenate(parts, axis=0))
    for step in range(1, groups):
        places.append(table[shifted(-step)])
    flat = jnp.concatenate(pieces, axis=1)
    place_of = jnp.concatenate(places, axis=0)
    pick = (mine[:, None] == place_of[None, :]).astype(jnp.bfloat16)
    total = jnp.einsum("st,tab->sab", pick, flat, preferred_element_type=jnp.float32)
    fresh = (old.astype(jnp.float32) - total).astype(jnp.bfloat16)
    back = lax.all_to_all(fresh, "own", split_axis=0, concat_axis=0, tiled=True)
    new_core_t = apply_grads(core_t, jnp.transpose(flat, (1, 0, 2)), (place_of - grp * per_device)[:, None])
    new_core = jnp.transpose(new_core_t, (2, 0, 1))
    new_left = jnp.einsum(
        "sea,sab->seb", left, unpack(back[slot_of_tile]), preferred_element_type=jnp.float32
    ).astype(jnp.bfloat16)
    return new_core, new_left


def solution(mesh):
    tiles = P(("grp", "own"), None, None)
    return jax.shard_map(
        body,
        mesh=mesh,
        in_specs=(tiles, tiles, P(("grp", "own"), None), tiles, P(("grp", "own")), P(("grp", "own"))),
        out_specs=(tiles, tiles),
        check_vma=False,
    )
```

```python
import functools

import jax
import jax.numpy as jnp
from jax import lax
from jax.experimental import pallas as pl
from jax.experimental.pallas import tpu as pltpu
from jax.sharding import PartitionSpec as P


def pack(x):
    half = x.shape[-2] // 2
    return jnp.concatenate([x[..., :half, :], x[..., half:, :]], axis=-1)


def unpack(x):
    half = x.shape[-1] // 2
    return jnp.concatenate([x[..., :half], x[..., half:]], axis=-2)


def one_hot(places, width):
    lanes = lax.broadcasted_iota(jnp.int32, (places.shape[0], width), 1)
    return (places == lanes).astype(jnp.float32).astype(jnp.bfloat16)


def fetch_kernel(place_ref, core_ref, out_ref):
    half = out_ref.shape[0]
    hot = one_hot(place_ref[...], core_ref.shape[2])

    def step(i, carry):
        slab = jnp.concatenate([core_ref[i], core_ref[i + half]], axis=0)
        out_ref[i] = lax.dot_general(
            hot, slab, (((1,), (1,)), ((), ())), preferred_element_type=jnp.float32
        ).astype(out_ref.dtype)
        return carry

    lax.fori_loop(0, half, step, 0, unroll=2)


def fetch(core_t, places):
    rank, _, count = core_t.shape
    wanted = places.shape[0]
    return pl.pallas_call(
        fetch_kernel,
        out_shape=jax.ShapeDtypeStruct((rank // 2, wanted, 2 * rank), core_t.dtype),
        compiler_params=pltpu.CompilerParams(vmem_limit_bytes=48 * 2**20),
        cost_estimate=pl.CostEstimate(
            flops=2 * wanted * count * rank * rank, bytes_accessed=2 * rank * rank * (count + wanted), transcendentals=0
        ),
    )(places, core_t)


def apply_kernel(place_ref, core_ref, grads_ref, out_ref):
    half = grads_ref.shape[0]
    rank = out_ref.shape[1]
    hot = one_hot(place_ref[...], core_ref.shape[2])

    def step(i, carry):
        total = lax.dot_general(
            grads_ref[i], hot, (((0,), (0,)), ((), ())), preferred_element_type=jnp.float32
        )
        for part, row in ((0, i), (1, i + half)):
            change = total[part * rank:(part + 1) * rank]
            out_ref[row] = (core_ref[row].astype(jnp.float32) - change).astype(out_ref.dtype)
        return carry

    lax.fori_loop(0, half, step, 0, unroll=2)


def apply_grads(core_t, grads, places):
    rank, _, count = core_t.shape
    wanted = places.shape[0]
    return pl.pallas_call(
        apply_kernel,
        out_shape=jax.ShapeDtypeStruct(core_t.shape, core_t.dtype),
        compiler_params=pltpu.CompilerParams(vmem_limit_bytes=48 * 2**20),
        cost_estimate=pl.CostEstimate(
            flops=2 * wanted * count * rank * rank,
            bytes_accessed=2 * rank * rank * (2 * count + wanted),
            transcendentals=0,
        ),
    )(places, core_t, grads)


MESH = pl.DeviceIdType.MESH


def greet(groups, owners):
    grp, own = lax.axis_index("grp"), lax.axis_index("own")
    barrier = pltpu.get_barrier_semaphore()
    for step in range(1, groups):
        pl.semaphore_signal(barrier, inc=1, device_id=(lax.rem(grp + step, groups), own), device_id_type=MESH)

    def hail(i, carry):
        pl.semaphore_signal(barrier, inc=1, device_id=(grp, lax.rem(own + i + 1, owners)), device_id_type=MESH)
        return carry

    lax.fori_loop(0, owners - 1, hail, 0)
    pl.semaphore_wait(barrier, groups + owners - 2)


def deliver_kernel(groups, owners, rows, old, out, inbox, cross_send, cross_recv, send_sem, recv_sem):
    grp, own = lax.axis_index("grp"), lax.axis_index("own")
    slots = old.shape[0]
    cap = slots // owners
    greet(groups, owners)

    def cross(step, i):
        start = lax.rem(own + i + 1, owners) * cap
        return pltpu.make_async_remote_copy(
            src_ref=rows.at[pl.ds(step * slots + start, cap)],
            dst_ref=inbox.at[step - 1, pl.ds(start, cap)],
            send_sem=cross_send.at[step - 1, i],
            recv_sem=cross_recv.at[step - 1, i],
            device_id=(lax.rem(grp + step, groups), own),
            device_id_type=MESH,
        )

    def along(i):
        peer = lax.rem(own + i + 1, owners)
        return pltpu.make_async_remote_copy(
            src_ref=old.at[pl.ds(peer * cap, cap)],
            dst_ref=out.at[pl.ds(own * cap, cap)],
            send_sem=send_sem.at[i],
            recv_sem=recv_sem.at[i],
            device_id=(grp, peer),
            device_id_type=MESH,
        )

    def launch(i, carry):
        for step in range(1, groups):
            cross(step, i).start()
        return carry

    def merge(i):
        start = lax.rem(own + i + 1, owners) * cap
        total = rows[pl.ds(start, cap)]
        for step in range(1, groups):
            cross(step, i).wait_recv()
            total = total + inbox[step - 1, pl.ds(start, cap)]
        old[pl.ds(start, cap)] = total
        return total

    def forward(i, carry):
        merge(i)
        along(i).start()
        return carry

    def drain(i, carry):
        along(i).wait()
        return carry

    def drain_cross(i, carry):
        for step in range(1, groups):
            cross(step, i).wait_send()
        return carry

    lax.fori_loop(0, owners, launch, 0)
    lax.fori_loop(0, owners - 1, forward, 0)
    out[pl.ds(own * cap, cap)] = merge(owners - 1)
    lax.fori_loop(0, owners, drain_cross, 0)
    lax.fori_loop(0, owners - 1, drain, 0)


def deliver(rows, groups, owners):
    slots = rows.shape[0] // groups
    shape = (slots,) + rows.shape[1:]
    return pl.pallas_call(
        functools.partial(deliver_kernel, groups, owners),
        out_shape=[jax.ShapeDtypeStruct(shape, rows.dtype)] * 2,
        in_specs=[pl.BlockSpec(memory_space=pltpu.VMEM)],
        out_specs=[pl.BlockSpec(memory_space=pltpu.VMEM)] * 2,
        scratch_shapes=[
            pltpu.VMEM((groups - 1,) + shape, rows.dtype),
            pltpu.SemaphoreType.DMA((groups - 1, owners)),
            pltpu.SemaphoreType.DMA((groups - 1, owners)),
            pltpu.SemaphoreType.DMA((owners - 1,)),
            pltpu.SemaphoreType.DMA((owners - 1,)),
        ],
        compiler_params=pltpu.CompilerParams(
            collective_id=1, has_side_effects=True, vmem_limit_bytes=48 * 2**20
        ),
    )(rows)


def collect_kernel(groups, owners, send, flat, cross_send, cross_recv, send_sem, recv_sem):
    grp, own = lax.axis_index("grp"), lax.axis_index("own")
    slots = send.shape[0]
    cap = slots // owners
    greet(groups, owners)

    def along(i):
        peer = lax.rem(own + i + 1, owners)
        return pltpu.make_async_remote_copy(
            src_ref=send.at[pl.ds(peer * cap, cap)],
            dst_ref=flat.at[pl.ds(own * cap, cap)],
            send_sem=send_sem.at[i],
            recv_sem=recv_sem.at[i],
            device_id=(grp, peer),
            device_id_type=MESH,
        )

    def cross(step, i):
        start = lax.rem(own - i - 1 + owners, owners) * cap
        return pltpu.make_async_remote_copy(
            src_ref=flat.at[pl.ds(start, cap)],
            dst_ref=flat.at[pl.ds(step * slots + start, cap)],
            send_sem=cross_send.at[step - 1, i],
            recv_sem=cross_recv.at[step - 1, i],
            device_id=(lax.rem(grp + step, groups), own),
            device_id_type=MESH,
        )

    def launch(i, carry):
        along(i).start()
        return carry

    def share(i):
        for step in range(1, groups):
            cross(step, i).start()

    def forward(i, carry):
        along(i).wait_recv()
        share(i)
        return carry

    def drain(i, carry):
        along(i).wait_send()
        return carry

    def drain_cross(i, carry):
        for step in range(1, groups):
            cross(step, i).wait()
        return carry

    lax.fori_loop(0, owners - 1, launch, 0)
    flat[pl.ds(own * cap, cap)] = send[pl.ds(own * cap, cap)]
    share(owners - 1)
    lax.fori_loop(0, owners - 1, forward, 0)
    lax.fori_loop(0, owners - 1, drain, 0)
    lax.fori_loop(0, owners, drain_cross, 0)


def collect(send, groups, owners):
    slots = send.shape[0]
    return pl.pallas_call(
        functools.partial(collect_kernel, groups, owners),
        out_shape=jax.ShapeDtypeStruct((groups * slots,) + send.shape[1:], send.dtype),
        in_specs=[pl.BlockSpec(memory_space=pltpu.VMEM)],
        out_specs=pl.BlockSpec(memory_space=pltpu.VMEM),
        scratch_shapes=[
            pltpu.SemaphoreType.DMA((groups - 1, owners)),
            pltpu.SemaphoreType.DMA((groups - 1, owners)),
            pltpu.SemaphoreType.DMA((owners - 1,)),
            pltpu.SemaphoreType.DMA((owners - 1,)),
        ],
        compiler_params=pltpu.CompilerParams(
            collective_id=2, has_side_effects=True, vmem_limit_bytes=48 * 2**20
        ),
    )(send)


def body(left, right, values, core, tile_slice, tile_fill):
    owners = lax.axis_size("own")
    groups = lax.axis_size("grp")
    tile_count, tile_rows, rank = left.shape
    per_device = core.shape[0]
    cap = 2 * tile_count // owners
    slots = owners * cap
    grp = lax.axis_index("grp")
    block = tile_slice // per_device
    owner = block % owners
    place = block // owners * per_device + tile_slice % per_device
    pos = jnp.arange(tile_count)
    earlier = (owner[:, None] == owner[None, :]) & (pos[None, :] < pos[:, None])
    slot_of_tile = owner * cap + jnp.sum(earlier.astype(jnp.int32), axis=1)
    match = slot_of_tile[None, :] == jnp.arange(slots)[:, None]
    live = jnp.any(match, axis=1)
    tile_of_slot = jnp.sum(jnp.where(match, pos[None, :], 0), axis=1)
    want = jnp.sum(jnp.where(match, place[None, :] + 1, 0), axis=1) - 1
    table = lax.all_to_all(
        jnp.broadcast_to(want.reshape(1, owners, cap), (groups, owners, cap)).reshape(groups * owners, cap),
        ("grp", "own"), split_axis=0, concat_axis=0, tiled=True,
    ).reshape(groups, slots)

    def shifted(step):
        return (grp + step) % groups

    core_t = jnp.transpose(core, (1, 2, 0))
    local = table - grp * per_device
    mine = table[grp]
    order = [shifted(step) for step in range(groups)]
    found = fetch(core_t, jnp.concatenate([local[g] for g in order])[:, None])
    old, slices = deliver(jnp.transpose(found, (1, 0, 2)), groups, owners)
    tables = unpack(slices[slot_of_tile])

    projected = jnp.einsum("sea,sab->seb", left, tables, preferred_element_type=jnp.float32)
    predicted = jnp.sum(projected * right.astype(jnp.float32), axis=-1)
    live_rows = jnp.arange(tile_rows)[None, :] < tile_fill[:, None]
    residual = jnp.where(live_rows, predicted - values.astype(jnp.float32), 0.0)
    weighted = (residual[:, :, None] * left.astype(jnp.float32)).astype(jnp.bfloat16)
    grad = jnp.einsum("sea,seb->sab", weighted, right, preferred_element_type=jnp.float32).astype(jnp.bfloat16)
    send = jnp.where(live[:, None, None], pack(grad)[tile_of_slot], jnp.bfloat16(0))
    flat = collect(send, groups, owners)
    places = [mine]
    for step in range(1, groups):
        places.append(table[shifted(-step)])
    place_of = jnp.concatenate(places, axis=0)
    pick = (mine[:, None] == place_of[None, :]).astype(jnp.bfloat16)
    total = jnp.einsum("st,tab->sab", pick, flat, preferred_element_type=jnp.float32)
    fresh = (old.astype(jnp.float32) - total).astype(jnp.bfloat16)
    back = lax.all_to_all(fresh, "own", split_axis=0, concat_axis=0, tiled=True)
    new_core_t = apply_grads(core_t, jnp.transpose(flat, (1, 0, 2)), (place_of - grp * per_device)[:, None])
    new_core = jnp.transpose(new_core_t, (2, 0, 1))
    new_left = jnp.einsum(
        "sea,sab->seb", left, unpack(back[slot_of_tile]), preferred_element_type=jnp.float32
    ).astype(jnp.bfloat16)
    return new_core, new_left


def solution(mesh):
    tiles = P(("grp", "own"), None, None)
    return jax.shard_map(
        body,
        mesh=mesh,
        in_specs=(tiles, tiles, P(("grp", "own"), None), tiles, P(("grp", "own")), P(("grp", "own"))),
        out_specs=(tiles, tiles),
        check_vma=False,
    )
```

```python
import functools

import jax
import jax.numpy as jnp
from jax import lax
from jax.experimental import pallas as pl
from jax.experimental.pallas import tpu as pltpu
from jax.sharding import PartitionSpec as P


def pack(x):
    half = x.shape[-2] // 2
    return jnp.concatenate([x[..., :half, :], x[..., half:, :]], axis=-1)


def unpack(x):
    half = x.shape[-1] // 2
    return jnp.concatenate([x[..., :half], x[..., half:]], axis=-2)


def one_hot(places, width):
    lanes = lax.broadcasted_iota(jnp.int32, (places.shape[0], width), 1)
    return (places == lanes).astype(jnp.float32).astype(jnp.bfloat16)


def fetch_kernel(place_ref, core_ref, out_ref):
    half = out_ref.shape[0]
    hot = one_hot(place_ref[...], core_ref.shape[2])

    def step(i, carry):
        slab = jnp.concatenate([core_ref[i], core_ref[i + half]], axis=0)
        out_ref[i] = lax.dot_general(
            hot, slab, (((1,), (1,)), ((), ())), preferred_element_type=jnp.float32
        ).astype(out_ref.dtype)
        return carry

    lax.fori_loop(0, half, step, 0, unroll=2)


def fetch(core_t, places):
    rank, _, count = core_t.shape
    wanted = places.shape[0]
    return pl.pallas_call(
        fetch_kernel,
        out_shape=jax.ShapeDtypeStruct((rank // 2, wanted, 2 * rank), core_t.dtype),
        compiler_params=pltpu.CompilerParams(vmem_limit_bytes=48 * 2**20),
        cost_estimate=pl.CostEstimate(
            flops=2 * wanted * count * rank * rank, bytes_accessed=2 * rank * rank * (count + wanted), transcendentals=0
        ),
    )(places, core_t)


MESH = pl.DeviceIdType.MESH
LANES = 128


def greet(groups, owners):
    grp, own = lax.axis_index("grp"), lax.axis_index("own")
    barrier = pltpu.get_barrier_semaphore()
    for step in range(1, groups):
        pl.semaphore_signal(barrier, inc=1, device_id=(lax.rem(grp + step, groups), own), device_id_type=MESH)

    def hail(i, carry):
        pl.semaphore_signal(barrier, inc=1, device_id=(grp, lax.rem(own + i + 1, owners)), device_id_type=MESH)
        return carry

    lax.fori_loop(0, owners - 1, hail, 0)
    pl.semaphore_wait(barrier, groups + owners - 2)


def deliver_kernel(groups, owners, rows, old, out, inbox, cross_send, cross_recv, send_sem, recv_sem):
    grp, own = lax.axis_index("grp"), lax.axis_index("own")
    slots = old.shape[0]
    cap = slots // owners
    greet(groups, owners)

    def cross(step, i):
        start = lax.rem(own + i + 1, owners) * cap
        return pltpu.make_async_remote_copy(
            src_ref=rows.at[pl.ds(step * slots + start, cap)],
            dst_ref=inbox.at[step - 1, pl.ds(start, cap)],
            send_sem=cross_send.at[step - 1, i],
            recv_sem=cross_recv.at[step - 1, i],
            device_id=(lax.rem(grp + step, groups), own),
            device_id_type=MESH,
        )

    def along(i):
        peer = lax.rem(own + i + 1, owners)
        return pltpu.make_async_remote_copy(
            src_ref=old.at[pl.ds(peer * cap, cap)],
            dst_ref=out.at[pl.ds(own * cap, cap)],
            send_sem=send_sem.at[i],
            recv_sem=recv_sem.at[i],
            device_id=(grp, peer),
            device_id_type=MESH,
        )

    def launch(i, carry):
        for step in range(1, groups):
            cross(step, i).start()
        return carry

    def merge(i):
        start = lax.rem(own + i + 1, owners) * cap
        total = rows[pl.ds(start, cap)]
        for step in range(1, groups):
            cross(step, i).wait_recv()
            total = total + inbox[step - 1, pl.ds(start, cap)]
        old[pl.ds(start, cap)] = total
        return total

    def forward(i, carry):
        merge(i)
        along(i).start()
        return carry

    def drain(i, carry):
        along(i).wait()
        return carry

    def drain_cross(i, carry):
        for step in range(1, groups):
            cross(step, i).wait_send()
        return carry

    lax.fori_loop(0, owners, launch, 0)
    lax.fori_loop(0, owners - 1, forward, 0)
    out[pl.ds(own * cap, cap)] = merge(owners - 1)
    lax.fori_loop(0, owners, drain_cross, 0)
    lax.fori_loop(0, owners - 1, drain, 0)


def deliver(rows, groups, owners):
    slots = rows.shape[0] // groups
    shape = (slots,) + rows.shape[1:]
    return pl.pallas_call(
        functools.partial(deliver_kernel, groups, owners),
        out_shape=[jax.ShapeDtypeStruct(shape, rows.dtype)] * 2,
        in_specs=[pl.BlockSpec(memory_space=pltpu.VMEM)],
        out_specs=[pl.BlockSpec(memory_space=pltpu.VMEM)] * 2,
        scratch_shapes=[
            pltpu.VMEM((groups - 1,) + shape, rows.dtype),
            pltpu.SemaphoreType.DMA((groups - 1, owners)),
            pltpu.SemaphoreType.DMA((groups - 1, owners)),
            pltpu.SemaphoreType.DMA((owners - 1,)),
            pltpu.SemaphoreType.DMA((owners - 1,)),
        ],
        compiler_params=pltpu.CompilerParams(
            collective_id=1, has_side_effects=True, vmem_limit_bytes=48 * 2**20
        ),
    )(rows)


def collect_kernel(groups, owners, send, flat, cross_send, cross_recv, send_sem, recv_sem):
    grp, own = lax.axis_index("grp"), lax.axis_index("own")
    slots = send.shape[0]
    cap = slots // owners
    greet(groups, owners)

    def along(i):
        peer = lax.rem(own + i + 1, owners)
        return pltpu.make_async_remote_copy(
            src_ref=send.at[pl.ds(peer * cap, cap)],
            dst_ref=flat.at[pl.ds(own * cap, cap)],
            send_sem=send_sem.at[i],
            recv_sem=recv_sem.at[i],
            device_id=(grp, peer),
            device_id_type=MESH,
        )

    def cross(step, i):
        start = lax.rem(own - i - 1 + owners, owners) * cap
        return pltpu.make_async_remote_copy(
            src_ref=flat.at[pl.ds(start, cap)],
            dst_ref=flat.at[pl.ds(step * slots + start, cap)],
            send_sem=cross_send.at[step - 1, i],
            recv_sem=cross_recv.at[step - 1, i],
            device_id=(lax.rem(grp + step, groups), own),
            device_id_type=MESH,
        )

    def launch(i, carry):
        along(i).start()
        return carry

    def share(i):
        for step in range(1, groups):
            cross(step, i).start()

    def forward(i, carry):
        along(i).wait_recv()
        share(i)
        return carry

    def drain(i, carry):
        along(i).wait_send()
        return carry

    def drain_cross(i, carry):
        for step in range(1, groups):
            cross(step, i).wait()
        return carry

    lax.fori_loop(0, owners - 1, launch, 0)
    flat[pl.ds(own * cap, cap)] = send[pl.ds(own * cap, cap)]
    share(owners - 1)
    lax.fori_loop(0, owners - 1, forward, 0)
    lax.fori_loop(0, owners - 1, drain, 0)
    lax.fori_loop(0, owners, drain_cross, 0)


def collect(send, groups, owners):
    slots = send.shape[0]
    return pl.pallas_call(
        functools.partial(collect_kernel, groups, owners),
        out_shape=jax.ShapeDtypeStruct((groups * slots,) + send.shape[1:], send.dtype),
        in_specs=[pl.BlockSpec(memory_space=pltpu.VMEM)],
        out_specs=pl.BlockSpec(memory_space=pltpu.VMEM),
        scratch_shapes=[
            pltpu.SemaphoreType.DMA((groups - 1, owners)),
            pltpu.SemaphoreType.DMA((groups - 1, owners)),
            pltpu.SemaphoreType.DMA((owners - 1,)),
            pltpu.SemaphoreType.DMA((owners - 1,)),
        ],
        compiler_params=pltpu.CompilerParams(
            collective_id=2, has_side_effects=True, vmem_limit_bytes=48 * 2**20
        ),
    )(send)


def swap_kernel(groups, owners, want, out, send_sem, recv_sem):
    grp, own = lax.axis_index("grp"), lax.axis_index("own")
    everyone = groups * owners
    me = grp * owners + own
    barrier = pltpu.get_barrier_semaphore()

    def peer(i):
        other = lax.rem(me + i + 1, everyone)
        return other // owners, lax.rem(other, owners)

    def hail(i, carry):
        pl.semaphore_signal(barrier, inc=1, device_id=peer(i), device_id_type=MESH)
        return carry

    def copy(i):
        to = peer(i)
        return pltpu.make_async_remote_copy(
            src_ref=want.at[to[1]],
            dst_ref=out.at[me],
            send_sem=send_sem.at[i],
            recv_sem=recv_sem.at[i],
            device_id=to,
            device_id_type=MESH,
        )

    def launch(i, carry):
        copy(i).start()
        return carry

    def drain(i, carry):
        copy(i).wait()
        return carry

    lax.fori_loop(0, everyone - 1, hail, 0)
    pl.semaphore_wait(barrier, everyone - 1)
    lax.fori_loop(0, everyone - 1, launch, 0)
    out[me] = want[own]
    lax.fori_loop(0, everyone - 1, drain, 0)


def swap(want, groups, owners):
    everyone = groups * owners
    return pl.pallas_call(
        functools.partial(swap_kernel, groups, owners),
        out_shape=jax.ShapeDtypeStruct((everyone,) + want.shape[1:], want.dtype),
        in_specs=[pl.BlockSpec(memory_space=pltpu.VMEM)],
        out_specs=pl.BlockSpec(memory_space=pltpu.VMEM),
        scratch_shapes=[pltpu.SemaphoreType.DMA((everyone - 1,)), pltpu.SemaphoreType.DMA((everyone - 1,))],
        compiler_params=pltpu.CompilerParams(collective_id=3, has_side_effects=True),
    )(want)


def finish_kernel(owners, place_ref, core_ref, grads_ref, fresh, out_ref, back, send_sem, recv_sem):
    grp, own = lax.axis_index("grp"), lax.axis_index("own")
    cap = fresh.shape[0] // owners
    half = grads_ref.shape[0]
    rank = out_ref.shape[1]
    greet(1, owners)

    def along(i):
        peer = lax.rem(own + i + 1, owners)
        return pltpu.make_async_remote_copy(
            src_ref=fresh.at[pl.ds(peer * cap, cap)],
            dst_ref=back.at[pl.ds(own * cap, cap)],
            send_sem=send_sem.at[i],
            recv_sem=recv_sem.at[i],
            device_id=(grp, peer),
            device_id_type=MESH,
        )

    def launch(i, carry):
        along(i).start()
        return carry

    def drain(i, carry):
        along(i).wait()
        return carry

    lax.fori_loop(0, owners - 1, launch, 0)
    back[pl.ds(own * cap, cap)] = fresh[pl.ds(own * cap, cap)]
    hot = one_hot(place_ref[...], core_ref.shape[2])

    def step(i, carry):
        total = lax.dot_general(
            grads_ref[i], hot, (((0,), (0,)), ((), ())), preferred_element_type=jnp.float32
        )
        for part, row in ((0, i), (1, i + half)):
            change = total[part * rank:(part + 1) * rank]
            out_ref[row] = (core_ref[row].astype(jnp.float32) - change).astype(out_ref.dtype)
        return carry

    lax.fori_loop(0, half, step, 0)
    lax.fori_loop(0, owners - 1, drain, 0)


def finish(core_t, grads, places, fresh, owners):
    return pl.pallas_call(
        functools.partial(finish_kernel, owners),
        out_shape=[
            jax.ShapeDtypeStruct(core_t.shape, core_t.dtype),
            jax.ShapeDtypeStruct(fresh.shape, fresh.dtype),
        ],
        in_specs=[pl.BlockSpec(memory_space=pltpu.VMEM)] * 4,
        out_specs=[pl.BlockSpec(memory_space=pltpu.VMEM)] * 2,
        scratch_shapes=[pltpu.SemaphoreType.DMA((owners - 1,)), pltpu.SemaphoreType.DMA((owners - 1,))],
        compiler_params=pltpu.CompilerParams(
            collective_id=4, has_side_effects=True, vmem_limit_bytes=48 * 2**20
        ),
    )(places, core_t, grads, fresh)


def body(left, right, values, core, tile_slice, tile_fill):
    owners = lax.axis_size("own")
    groups = lax.axis_size("grp")
    tile_count, tile_rows, rank = left.shape
    per_device = core.shape[0]
    cap = 2 * tile_count // owners
    slots = owners * cap
    grp = lax.axis_index("grp")
    block = tile_slice // per_device
    owner = block % owners
    place = block // owners * per_device + tile_slice % per_device
    pos = jnp.arange(tile_count)
    earlier = (owner[:, None] == owner[None, :]) & (pos[None, :] < pos[:, None])
    slot_of_tile = owner * cap + jnp.sum(earlier.astype(jnp.int32), axis=1)
    match = slot_of_tile[None, :] == jnp.arange(slots)[:, None]
    live = jnp.any(match, axis=1)
    tile_of_slot = jnp.sum(jnp.where(match, pos[None, :], 0), axis=1)
    want = jnp.sum(jnp.where(match, place[None, :] + 1, 0), axis=1) - 1
    wide = jnp.broadcast_to(want.reshape(owners, cap, 1), (owners, cap, LANES))
    table = swap(wide, groups, owners)[:, :, 0].reshape(groups, slots)

    def shifted(step):
        return (grp + step) % groups

    core_t = jnp.transpose(core, (1, 2, 0))
    local = table - grp * per_device
    mine = table[grp]
    order = [shifted(step) for step in range(groups)]
    found = fetch(core_t, jnp.concatenate([local[g] for g in order])[:, None])
    old, slices = deliver(jnp.transpose(found, (1, 0, 2)), groups, owners)
    tables = unpack(slices[slot_of_tile])

    projected = jnp.einsum("sea,sab->seb", left, tables, preferred_element_type=jnp.float32)
    predicted = jnp.sum(projected * right.astype(jnp.float32), axis=-1)
    live_rows = jnp.arange(tile_rows)[None, :] < tile_fill[:, None]
    residual = jnp.where(live_rows, predicted - values.astype(jnp.float32), 0.0)
    weighted = (residual[:, :, None] * left.astype(jnp.float32)).astype(jnp.bfloat16)
    grad = jnp.einsum("sea,seb->sab", weighted, right, preferred_element_type=jnp.float32).astype(jnp.bfloat16)
    send = jnp.where(live[:, None, None], pack(grad)[tile_of_slot], jnp.bfloat16(0))
    flat = collect(send, groups, owners)
    places = [mine]
    for step in range(1, groups):
        places.append(table[shifted(-step)])
    place_of = jnp.concatenate(places, axis=0)
    pick = (mine[:, None] == place_of[None, :]).astype(jnp.bfloat16)
    total = jnp.einsum("st,tab->sab", pick, flat, preferred_element_type=jnp.float32)
    fresh = (old.astype(jnp.float32) - total).astype(jnp.bfloat16)
    new_core_t, back = finish(
        core_t, jnp.transpose(flat, (1, 0, 2)), (place_of - grp * per_device)[:, None], fresh, owners
    )
    new_core = jnp.transpose(new_core_t, (2, 0, 1))
    new_left = jnp.einsum(
        "sea,sab->seb", left, unpack(back[slot_of_tile]), preferred_element_type=jnp.float32
    ).astype(jnp.bfloat16)
    return new_core, new_left


def solution(mesh):
    tiles = P(("grp", "own"), None, None)
    return jax.shard_map(
        body,
        mesh=mesh,
        in_specs=(tiles, tiles, P(("grp", "own"), None), tiles, P(("grp", "own")), P(("grp", "own"))),
        out_specs=(tiles, tiles),
        check_vma=False,
    )
```

```python
import functools

import jax
import jax.numpy as jnp
from jax import lax
from jax.experimental import pallas as pl
from jax.experimental.pallas import tpu as pltpu
from jax.sharding import PartitionSpec as P


def pack(x):
    half = x.shape[-2] // 2
    return jnp.concatenate([x[..., :half, :], x[..., half:, :]], axis=-1)


def unpack(x):
    half = x.shape[-1] // 2
    return jnp.concatenate([x[..., :half], x[..., half:]], axis=-2)


def one_hot(places, width):
    lanes = lax.broadcasted_iota(jnp.int32, (places.shape[0], width), 1)
    return (places == lanes).astype(jnp.float32).astype(jnp.bfloat16)


def fetch_kernel(place_ref, core_ref, out_ref):
    half = out_ref.shape[0]
    hot = one_hot(place_ref[...], core_ref.shape[2])

    def step(i, carry):
        slab = jnp.concatenate([core_ref[i], core_ref[i + half]], axis=0)
        out_ref[i] = lax.dot_general(
            hot, slab, (((1,), (1,)), ((), ())), preferred_element_type=jnp.float32
        ).astype(out_ref.dtype)
        return carry

    lax.fori_loop(0, half, step, 0, unroll=2)


def fetch(core_t, places):
    rank, _, count = core_t.shape
    wanted = places.shape[0]
    return pl.pallas_call(
        fetch_kernel,
        out_shape=jax.ShapeDtypeStruct((rank // 2, wanted, 2 * rank), core_t.dtype),
        compiler_params=pltpu.CompilerParams(vmem_limit_bytes=48 * 2**20),
        cost_estimate=pl.CostEstimate(
            flops=2 * wanted * count * rank * rank, bytes_accessed=2 * rank * rank * (count + wanted), transcendentals=0
        ),
    )(places, core_t)


MESH = pl.DeviceIdType.MESH
LANES = 128


def route(own, i, owners):
    if owners % 2:
        return lax.rem(own + i + 1, owners), lax.rem(own - i - 1 + owners, owners)
    half = owners // 2
    near = i // half
    base = lax.rem(own // half + 1 - near, 2) * half
    place = lax.rem(own, half)
    return base + lax.rem(place + i + near, half), base + lax.rem(place - i - near + owners, half)


def greet(groups, owners):
    grp, own = lax.axis_index("grp"), lax.axis_index("own")
    barrier = pltpu.get_barrier_semaphore()
    for step in range(1, groups):
        pl.semaphore_signal(barrier, inc=1, device_id=(lax.rem(grp + step, groups), own), device_id_type=MESH)

    def hail(i, carry):
        pl.semaphore_signal(barrier, inc=1, device_id=(grp, lax.rem(own + i + 1, owners)), device_id_type=MESH)
        return carry

    lax.fori_loop(0, owners - 1, hail, 0)
    pl.semaphore_wait(barrier, groups + owners - 2)


def deliver_kernel(groups, owners, rows, old, out, inbox, cross_send, cross_recv, send_sem, recv_sem):
    grp, own = lax.axis_index("grp"), lax.axis_index("own")
    slots = old.shape[0]
    cap = slots // owners
    greet(groups, owners)

    def cross(step, i):
        start = route(own, i, owners)[0] * cap
        return pltpu.make_async_remote_copy(
            src_ref=rows.at[pl.ds(step * slots + start, cap)],
            dst_ref=inbox.at[step - 1, pl.ds(start, cap)],
            send_sem=cross_send.at[step - 1, i],
            recv_sem=cross_recv.at[step - 1, i],
            device_id=(lax.rem(grp + step, groups), own),
            device_id_type=MESH,
        )

    def along(i):
        peer = route(own, i, owners)[0]
        return pltpu.make_async_remote_copy(
            src_ref=old.at[pl.ds(peer * cap, cap)],
            dst_ref=out.at[pl.ds(own * cap, cap)],
            send_sem=send_sem.at[i],
            recv_sem=recv_sem.at[i],
            device_id=(grp, peer),
            device_id_type=MESH,
        )

    def launch(i, carry):
        for step in range(1, groups):
            cross(step, i).start()
        return carry

    def merge(i):
        start = route(own, i, owners)[0] * cap
        total = rows[pl.ds(start, cap)]
        for step in range(1, groups):
            cross(step, i).wait_recv()
            total = total + inbox[step - 1, pl.ds(start, cap)]
        old[pl.ds(start, cap)] = total
        return total

    def forward(i, carry):
        merge(i)
        along(i).start()
        return carry

    def drain(i, carry):
        along(i).wait()
        return carry

    def drain_cross(i, carry):
        for step in range(1, groups):
            cross(step, i).wait_send()
        return carry

    lax.fori_loop(0, owners, launch, 0)
    lax.fori_loop(0, owners - 1, forward, 0)
    out[pl.ds(own * cap, cap)] = merge(owners - 1)
    lax.fori_loop(0, owners, drain_cross, 0)
    lax.fori_loop(0, owners - 1, drain, 0)


def deliver(rows, groups, owners):
    slots = rows.shape[0] // groups
    shape = (slots,) + rows.shape[1:]
    return pl.pallas_call(
        functools.partial(deliver_kernel, groups, owners),
        out_shape=[jax.ShapeDtypeStruct(shape, rows.dtype)] * 2,
        in_specs=[pl.BlockSpec(memory_space=pltpu.VMEM)],
        out_specs=[pl.BlockSpec(memory_space=pltpu.VMEM)] * 2,
        scratch_shapes=[
            pltpu.VMEM((groups - 1,) + shape, rows.dtype),
            pltpu.SemaphoreType.DMA((groups - 1, owners)),
            pltpu.SemaphoreType.DMA((groups - 1, owners)),
            pltpu.SemaphoreType.DMA((owners - 1,)),
            pltpu.SemaphoreType.DMA((owners - 1,)),
        ],
        compiler_params=pltpu.CompilerParams(
            collective_id=1, has_side_effects=True, vmem_limit_bytes=48 * 2**20
        ),
    )(rows)


def collect_kernel(groups, owners, send, flat, cross_send, cross_recv, send_sem, recv_sem):
    grp, own = lax.axis_index("grp"), lax.axis_index("own")
    slots = send.shape[0]
    cap = slots // owners
    greet(groups, owners)

    def turn(i):
        return i if owners % 2 else i // 2 + i % 2 * (owners // 2)

    def along(i):
        peer = route(own, turn(i), owners)[0]
        return pltpu.make_async_remote_copy(
            src_ref=send.at[pl.ds(peer * cap, cap)],
            dst_ref=flat.at[pl.ds(own * cap, cap)],
            send_sem=send_sem.at[i],
            recv_sem=recv_sem.at[i],
            device_id=(grp, peer),
            device_id_type=MESH,
        )

    def cross(step, i):
        start = route(own, turn(i), owners)[1] * cap
        return pltpu.make_async_remote_copy(
            src_ref=flat.at[pl.ds(start, cap)],
            dst_ref=flat.at[pl.ds(step * slots + start, cap)],
            send_sem=cross_send.at[step - 1, i],
            recv_sem=cross_recv.at[step - 1, i],
            device_id=(lax.rem(grp + step, groups), own),
            device_id_type=MESH,
        )

    def launch(i, carry):
        along(i).start()
        return carry

    def share(i):
        for step in range(1, groups):
            cross(step, i).start()

    def forward(i, carry):
        along(i).wait_recv()
        share(i)
        return carry

    def drain(i, carry):
        along(i).wait_send()
        return carry

    def drain_cross(i, carry):
        for step in range(1, groups):
            cross(step, i).wait()
        return carry

    lax.fori_loop(0, owners - 1, launch, 0)
    flat[pl.ds(own * cap, cap)] = send[pl.ds(own * cap, cap)]
    share(owners - 1)
    lax.fori_loop(0, owners - 1, forward, 0)
    lax.fori_loop(0, owners - 1, drain, 0)
    lax.fori_loop(0, owners, drain_cross, 0)


def collect(send, groups, owners):
    slots = send.shape[0]
    return pl.pallas_call(
        functools.partial(collect_kernel, groups, owners),
        out_shape=jax.ShapeDtypeStruct((groups * slots,) + send.shape[1:], send.dtype),
        in_specs=[pl.BlockSpec(memory_space=pltpu.VMEM)],
        out_specs=pl.BlockSpec(memory_space=pltpu.VMEM),
        scratch_shapes=[
            pltpu.SemaphoreType.DMA((groups - 1, owners)),
            pltpu.SemaphoreType.DMA((groups - 1, owners)),
            pltpu.SemaphoreType.DMA((owners - 1,)),
            pltpu.SemaphoreType.DMA((owners - 1,)),
        ],
        compiler_params=pltpu.CompilerParams(
            collective_id=2, has_side_effects=True, vmem_limit_bytes=48 * 2**20
        ),
    )(send)


def swap_kernel(groups, owners, want, out, send_sem, recv_sem):
    grp, own = lax.axis_index("grp"), lax.axis_index("own")
    everyone = groups * owners
    me = grp * owners + own
    barrier = pltpu.get_barrier_semaphore()

    def peer(i):
        other = lax.rem(me + i + 1, everyone)
        return other // owners, lax.rem(other, owners)

    def hail(i, carry):
        pl.semaphore_signal(barrier, inc=1, device_id=peer(i), device_id_type=MESH)
        return carry

    def copy(i):
        to = peer(i)
        return pltpu.make_async_remote_copy(
            src_ref=want.at[to[1]],
            dst_ref=out.at[me],
            send_sem=send_sem.at[i],
            recv_sem=recv_sem.at[i],
            device_id=to,
            device_id_type=MESH,
        )

    def launch(i, carry):
        copy(i).start()
        return carry

    def drain(i, carry):
        copy(i).wait()
        return carry

    lax.fori_loop(0, everyone - 1, hail, 0)
    pl.semaphore_wait(barrier, everyone - 1)
    lax.fori_loop(0, everyone - 1, launch, 0)
    out[me] = want[own]
    lax.fori_loop(0, everyone - 1, drain, 0)


def swap(want, groups, owners):
    everyone = groups * owners
    return pl.pallas_call(
        functools.partial(swap_kernel, groups, owners),
        out_shape=jax.ShapeDtypeStruct((everyone,) + want.shape[1:], want.dtype),
        in_specs=[pl.BlockSpec(memory_space=pltpu.VMEM)],
        out_specs=pl.BlockSpec(memory_space=pltpu.VMEM),
        scratch_shapes=[pltpu.SemaphoreType.DMA((everyone - 1,)), pltpu.SemaphoreType.DMA((everyone - 1,))],
        compiler_params=pltpu.CompilerParams(collective_id=3, has_side_effects=True),
    )(want)


def finish_kernel(owners, place_ref, core_ref, grads_ref, fresh, out_ref, back, send_sem, recv_sem):
    grp, own = lax.axis_index("grp"), lax.axis_index("own")
    cap = fresh.shape[0] // owners
    half = grads_ref.shape[0]
    rank = out_ref.shape[1]
    greet(1, owners)

    def along(i):
        peer = route(own, i, owners)[0]
        return pltpu.make_async_remote_copy(
            src_ref=fresh.at[pl.ds(peer * cap, cap)],
            dst_ref=back.at[pl.ds(own * cap, cap)],
            send_sem=send_sem.at[i],
            recv_sem=recv_sem.at[i],
            device_id=(grp, peer),
            device_id_type=MESH,
        )

    def launch(i, carry):
        along(i).start()
        return carry

    def drain(i, carry):
        along(i).wait()
        return carry

    lax.fori_loop(0, owners - 1, launch, 0)
    back[pl.ds(own * cap, cap)] = fresh[pl.ds(own * cap, cap)]
    hot = one_hot(place_ref[...], core_ref.shape[2])

    def step(i, carry):
        total = lax.dot_general(
            grads_ref[i], hot, (((0,), (0,)), ((), ())), preferred_element_type=jnp.float32
        )
        for part, row in ((0, i), (1, i + half)):
            change = total[part * rank:(part + 1) * rank]
            out_ref[row] = (core_ref[row].astype(jnp.float32) - change).astype(out_ref.dtype)
        return carry

    lax.fori_loop(0, half, step, 0)
    lax.fori_loop(0, owners - 1, drain, 0)


def finish(core_t, grads, places, fresh, owners):
    return pl.pallas_call(
        functools.partial(finish_kernel, owners),
        out_shape=[
            jax.ShapeDtypeStruct(core_t.shape, core_t.dtype),
            jax.ShapeDtypeStruct(fresh.shape, fresh.dtype),
        ],
        in_specs=[pl.BlockSpec(memory_space=pltpu.VMEM)] * 4,
        out_specs=[pl.BlockSpec(memory_space=pltpu.VMEM)] * 2,
        scratch_shapes=[pltpu.SemaphoreType.DMA((owners - 1,)), pltpu.SemaphoreType.DMA((owners - 1,))],
        compiler_params=pltpu.CompilerParams(
            collective_id=4, has_side_effects=True, vmem_limit_bytes=48 * 2**20
        ),
    )(places, core_t, grads, fresh)


def body(left, right, values, core, tile_slice, tile_fill):
    owners = lax.axis_size("own")
    groups = lax.axis_size("grp")
    tile_count, tile_rows, rank = left.shape
    per_device = core.shape[0]
    cap = 2 * tile_count // owners
    slots = owners * cap
    grp = lax.axis_index("grp")
    block = tile_slice // per_device
    owner = block % owners
    place = block // owners * per_device + tile_slice % per_device
    pos = jnp.arange(tile_count)
    earlier = (owner[:, None] == owner[None, :]) & (pos[None, :] < pos[:, None])
    slot_of_tile = owner * cap + jnp.sum(earlier.astype(jnp.int32), axis=1)
    match = slot_of_tile[None, :] == jnp.arange(slots)[:, None]
    live = jnp.any(match, axis=1)
    tile_of_slot = jnp.sum(jnp.where(match, pos[None, :], 0), axis=1)
    want = jnp.sum(jnp.where(match, place[None, :] + 1, 0), axis=1) - 1
    wide = jnp.broadcast_to(want.reshape(owners, cap, 1), (owners, cap, LANES))
    table = swap(wide, groups, owners)[:, :, 0].reshape(groups, slots)

    def shifted(step):
        return (grp + step) % groups

    core_t = jnp.transpose(core, (1, 2, 0))
    local = table - grp * per_device
    mine = table[grp]
    order = [shifted(step) for step in range(groups)]
    found = fetch(core_t, jnp.concatenate([local[g] for g in order])[:, None])
    old, slices = deliver(jnp.transpose(found, (1, 0, 2)), groups, owners)
    tables = unpack(slices[slot_of_tile])

    projected = jnp.einsum("sea,sab->seb", left, tables, preferred_element_type=jnp.float32)
    predicted = jnp.sum(projected * right.astype(jnp.float32), axis=-1)
    live_rows = jnp.arange(tile_rows)[None, :] < tile_fill[:, None]
    residual = jnp.where(live_rows, predicted - values.astype(jnp.float32), 0.0)
    weighted = (residual[:, :, None] * left.astype(jnp.float32)).astype(jnp.bfloat16)
    grad = jnp.einsum("sea,seb->sab", weighted, right, preferred_element_type=jnp.float32).astype(jnp.bfloat16)
    send = jnp.where(live[:, None, None], pack(grad)[tile_of_slot], jnp.bfloat16(0))
    flat = collect(send, groups, owners)
    places = [mine]
    for step in range(1, groups):
        places.append(table[shifted(-step)])
    place_of = jnp.concatenate(places, axis=0)
    pick = (mine[:, None] == place_of[None, :]).astype(jnp.bfloat16)
    total = jnp.einsum("st,tab->sab", pick, flat, preferred_element_type=jnp.float32)
    fresh = (old.astype(jnp.float32) - total).astype(jnp.bfloat16)
    new_core_t, back = finish(
        core_t, jnp.transpose(flat, (1, 0, 2)), (place_of - grp * per_device)[:, None], fresh, owners
    )
    new_core = jnp.transpose(new_core_t, (2, 0, 1))
    new_left = jnp.einsum(
        "sea,sab->seb", left, unpack(back[slot_of_tile]), preferred_element_type=jnp.float32
    ).astype(jnp.bfloat16)
    return new_core, new_left


def solution(mesh):
    tiles = P(("grp", "own"), None, None)
    return jax.shard_map(
        body,
        mesh=mesh,
        in_specs=(tiles, tiles, P(("grp", "own"), None), tiles, P(("grp", "own")), P(("grp", "own"))),
        out_specs=(tiles, tiles),
        check_vma=False,
    )
```

```python
import functools

import jax
import jax.numpy as jnp
from jax import lax
from jax.experimental import pallas as pl
from jax.experimental.pallas import tpu as pltpu
from jax.sharding import PartitionSpec as P


def pack(x):
    half = x.shape[-2] // 2
    return jnp.concatenate([x[..., :half, :], x[..., half:, :]], axis=-1)


def unpack(x):
    half = x.shape[-1] // 2
    return jnp.concatenate([x[..., :half], x[..., half:]], axis=-2)


def one_hot(places, width):
    lanes = lax.broadcasted_iota(jnp.int32, (places.shape[0], width), 1)
    return (places == lanes).astype(jnp.float32).astype(jnp.bfloat16)


def fetch_kernel(place_ref, core_ref, out_ref):
    half = out_ref.shape[0]
    hot = one_hot(place_ref[...], core_ref.shape[2])

    rank = core_ref.shape[1]

    def step(i, carry):
        row = 2 * i
        slab = jnp.concatenate(
            [core_ref[row], core_ref[row + half], core_ref[row + 1], core_ref[row + 1 + half]], axis=0
        )
        both = lax.dot_general(
            hot, slab, (((1,), (1,)), ((), ())), preferred_element_type=jnp.float32
        ).astype(out_ref.dtype)
        out_ref[row] = both[:, :2 * rank]
        out_ref[row + 1] = both[:, 2 * rank:]
        return carry

    lax.fori_loop(0, half // 2, step, 0, unroll=2)


def fetch(core_t, places):
    rank, _, count = core_t.shape
    wanted = places.shape[0]
    return pl.pallas_call(
        fetch_kernel,
        out_shape=jax.ShapeDtypeStruct((rank // 2, wanted, 2 * rank), core_t.dtype),
        compiler_params=pltpu.CompilerParams(vmem_limit_bytes=48 * 2**20),
        cost_estimate=pl.CostEstimate(
            flops=2 * wanted * count * rank * rank, bytes_accessed=2 * rank * rank * (count + wanted), transcendentals=0
        ),
    )(places, core_t)


MESH = pl.DeviceIdType.MESH
LANES = 128


def route(own, i, owners):
    if owners % 2:
        return lax.rem(own + i + 1, owners), lax.rem(own - i - 1 + owners, owners)
    half = owners // 2
    near = i // half
    base = lax.rem(own // half + 1 - near, 2) * half
    place = lax.rem(own, half)
    return base + lax.rem(place + i + near, half), base + lax.rem(place - i - near + owners, half)


def greet(groups, owners):
    grp, own = lax.axis_index("grp"), lax.axis_index("own")
    barrier = pltpu.get_barrier_semaphore()
    for step in range(1, groups):
        pl.semaphore_signal(barrier, inc=1, device_id=(lax.rem(grp + step, groups), own), device_id_type=MESH)

    def hail(i, carry):
        pl.semaphore_signal(barrier, inc=1, device_id=(grp, lax.rem(own + i + 1, owners)), device_id_type=MESH)
        return carry

    lax.fori_loop(0, owners - 1, hail, 0)
    pl.semaphore_wait(barrier, groups + owners - 2)


def deliver_kernel(groups, owners, rows, old, out, inbox, cross_send, cross_recv, send_sem, recv_sem):
    grp, own = lax.axis_index("grp"), lax.axis_index("own")
    slots = old.shape[0]
    cap = slots // owners
    greet(groups, owners)

    def cross(step, i):
        start = route(own, i, owners)[0] * cap
        return pltpu.make_async_remote_copy(
            src_ref=rows.at[pl.ds(step * slots + start, cap)],
            dst_ref=inbox.at[step - 1, pl.ds(start, cap)],
            send_sem=cross_send.at[step - 1, i],
            recv_sem=cross_recv.at[step - 1, i],
            device_id=(lax.rem(grp + step, groups), own),
            device_id_type=MESH,
        )

    def along(i):
        peer = route(own, i, owners)[0]
        return pltpu.make_async_remote_copy(
            src_ref=old.at[pl.ds(peer * cap, cap)],
            dst_ref=out.at[pl.ds(own * cap, cap)],
            send_sem=send_sem.at[i],
            recv_sem=recv_sem.at[i],
            device_id=(grp, peer),
            device_id_type=MESH,
        )

    def launch(i, carry):
        for step in range(1, groups):
            cross(step, i).start()
        return carry

    def merge(i):
        start = route(own, i, owners)[0] * cap
        total = rows[pl.ds(start, cap)]
        for step in range(1, groups):
            cross(step, i).wait_recv()
            total = total + inbox[step - 1, pl.ds(start, cap)]
        old[pl.ds(start, cap)] = total
        return total

    def forward(i, carry):
        merge(i)
        along(i).start()
        return carry

    def drain(i, carry):
        along(i).wait()
        return carry

    def drain_cross(i, carry):
        for step in range(1, groups):
            cross(step, i).wait_send()
        return carry

    lax.fori_loop(0, owners, launch, 0)
    lax.fori_loop(0, owners - 1, forward, 0)
    out[pl.ds(own * cap, cap)] = merge(owners - 1)
    lax.fori_loop(0, owners, drain_cross, 0)
    lax.fori_loop(0, owners - 1, drain, 0)


def deliver(rows, groups, owners):
    slots = rows.shape[0] // groups
    shape = (slots,) + rows.shape[1:]
    return pl.pallas_call(
        functools.partial(deliver_kernel, groups, owners),
        out_shape=[jax.ShapeDtypeStruct(shape, rows.dtype)] * 2,
        in_specs=[pl.BlockSpec(memory_space=pltpu.VMEM)],
        out_specs=[pl.BlockSpec(memory_space=pltpu.VMEM)] * 2,
        scratch_shapes=[
            pltpu.VMEM((groups - 1,) + shape, rows.dtype),
            pltpu.SemaphoreType.DMA((groups - 1, owners)),
            pltpu.SemaphoreType.DMA((groups - 1, owners)),
            pltpu.SemaphoreType.DMA((owners - 1,)),
            pltpu.SemaphoreType.DMA((owners - 1,)),
        ],
        compiler_params=pltpu.CompilerParams(
            collective_id=1, has_side_effects=True, vmem_limit_bytes=48 * 2**20
        ),
    )(rows)


def collect_kernel(groups, owners, send, flat, cross_send, cross_recv, send_sem, recv_sem):
    grp, own = lax.axis_index("grp"), lax.axis_index("own")
    slots = send.shape[0]
    cap = slots // owners
    greet(groups, owners)

    def turn(i):
        return i if owners % 2 else i // 2 + i % 2 * (owners // 2)

    def along(i):
        peer = route(own, turn(i), owners)[0]
        return pltpu.make_async_remote_copy(
            src_ref=send.at[pl.ds(peer * cap, cap)],
            dst_ref=flat.at[pl.ds(own * cap, cap)],
            send_sem=send_sem.at[i],
            recv_sem=recv_sem.at[i],
            device_id=(grp, peer),
            device_id_type=MESH,
        )

    def cross(step, i):
        start = route(own, turn(i), owners)[1] * cap
        return pltpu.make_async_remote_copy(
            src_ref=flat.at[pl.ds(start, cap)],
            dst_ref=flat.at[pl.ds(step * slots + start, cap)],
            send_sem=cross_send.at[step - 1, i],
            recv_sem=cross_recv.at[step - 1, i],
            device_id=(lax.rem(grp + step, groups), own),
            device_id_type=MESH,
        )

    def launch(i, carry):
        along(i).start()
        return carry

    def share(i):
        for step in range(1, groups):
            cross(step, i).start()

    def forward(i, carry):
        along(i).wait_recv()
        share(i)
        return carry

    def drain(i, carry):
        along(i).wait_send()
        return carry

    def drain_cross(i, carry):
        for step in range(1, groups):
            cross(step, i).wait()
        return carry

    lax.fori_loop(0, owners - 1, launch, 0)
    flat[pl.ds(own * cap, cap)] = send[pl.ds(own * cap, cap)]
    share(owners - 1)
    lax.fori_loop(0, owners - 1, forward, 0)
    lax.fori_loop(0, owners - 1, drain, 0)
    lax.fori_loop(0, owners, drain_cross, 0)


def collect(send, groups, owners):
    slots = send.shape[0]
    return pl.pallas_call(
        functools.partial(collect_kernel, groups, owners),
        out_shape=jax.ShapeDtypeStruct((groups * slots,) + send.shape[1:], send.dtype),
        in_specs=[pl.BlockSpec(memory_space=pltpu.VMEM)],
        out_specs=pl.BlockSpec(memory_space=pltpu.VMEM),
        scratch_shapes=[
            pltpu.SemaphoreType.DMA((groups - 1, owners)),
            pltpu.SemaphoreType.DMA((groups - 1, owners)),
            pltpu.SemaphoreType.DMA((owners - 1,)),
            pltpu.SemaphoreType.DMA((owners - 1,)),
        ],
        compiler_params=pltpu.CompilerParams(
            collective_id=2, has_side_effects=True, vmem_limit_bytes=48 * 2**20
        ),
    )(send)


def swap_kernel(groups, owners, want, out, send_sem, recv_sem):
    grp, own = lax.axis_index("grp"), lax.axis_index("own")
    everyone = groups * owners
    me = grp * owners + own
    barrier = pltpu.get_barrier_semaphore()

    def peer(i):
        other = lax.rem(me + i + 1, everyone)
        return other // owners, lax.rem(other, owners)

    def hail(i, carry):
        pl.semaphore_signal(barrier, inc=1, device_id=peer(i), device_id_type=MESH)
        return carry

    def copy(i):
        to = peer(i)
        return pltpu.make_async_remote_copy(
            src_ref=want.at[to[1]],
            dst_ref=out.at[me],
            send_sem=send_sem.at[i],
            recv_sem=recv_sem.at[i],
            device_id=to,
            device_id_type=MESH,
        )

    def launch(i, carry):
        copy(i).start()
        return carry

    def drain(i, carry):
        copy(i).wait()
        return carry

    lax.fori_loop(0, everyone - 1, hail, 0)
    pl.semaphore_wait(barrier, everyone - 1)
    lax.fori_loop(0, everyone - 1, launch, 0)
    out[me] = want[own]
    lax.fori_loop(0, everyone - 1, drain, 0)


def swap(want, groups, owners):
    everyone = groups * owners
    return pl.pallas_call(
        functools.partial(swap_kernel, groups, owners),
        out_shape=jax.ShapeDtypeStruct((everyone,) + want.shape[1:], want.dtype),
        in_specs=[pl.BlockSpec(memory_space=pltpu.VMEM)],
        out_specs=pl.BlockSpec(memory_space=pltpu.VMEM),
        scratch_shapes=[pltpu.SemaphoreType.DMA((everyone - 1,)), pltpu.SemaphoreType.DMA((everyone - 1,))],
        compiler_params=pltpu.CompilerParams(collective_id=3, has_side_effects=True),
    )(want)


def finish_kernel(owners, place_ref, core_ref, grads_ref, fresh, out_ref, back, send_sem, recv_sem):
    grp, own = lax.axis_index("grp"), lax.axis_index("own")
    cap = fresh.shape[0] // owners
    half = grads_ref.shape[0]
    rank = out_ref.shape[1]
    greet(1, owners)

    def along(i):
        peer = route(own, i, owners)[0]
        return pltpu.make_async_remote_copy(
            src_ref=fresh.at[pl.ds(peer * cap, cap)],
            dst_ref=back.at[pl.ds(own * cap, cap)],
            send_sem=send_sem.at[i],
            recv_sem=recv_sem.at[i],
            device_id=(grp, peer),
            device_id_type=MESH,
        )

    def launch(i, carry):
        along(i).start()
        return carry

    def drain(i, carry):
        along(i).wait()
        return carry

    lax.fori_loop(0, owners - 1, launch, 0)
    back[pl.ds(own * cap, cap)] = fresh[pl.ds(own * cap, cap)]
    hot = one_hot(place_ref[...], core_ref.shape[2])

    def step(i, carry):
        total = lax.dot_general(
            grads_ref[i], hot, (((0,), (0,)), ((), ())), preferred_element_type=jnp.float32
        )
        for part, row in ((0, i), (1, i + half)):
            change = total[part * rank:(part + 1) * rank]
            out_ref[row] = (core_ref[row].astype(jnp.float32) - change).astype(out_ref.dtype)
        return carry

    lax.fori_loop(0, half, step, 0)
    lax.fori_loop(0, owners - 1, drain, 0)


def finish(core_t, grads, places, fresh, owners):
    return pl.pallas_call(
        functools.partial(finish_kernel, owners),
        out_shape=[
            jax.ShapeDtypeStruct(core_t.shape, core_t.dtype),
            jax.ShapeDtypeStruct(fresh.shape, fresh.dtype),
        ],
        in_specs=[pl.BlockSpec(memory_space=pltpu.VMEM)] * 4,
        out_specs=[pl.BlockSpec(memory_space=pltpu.VMEM)] * 2,
        scratch_shapes=[pltpu.SemaphoreType.DMA((owners - 1,)), pltpu.SemaphoreType.DMA((owners - 1,))],
        compiler_params=pltpu.CompilerParams(
            collective_id=4, has_side_effects=True, vmem_limit_bytes=48 * 2**20
        ),
    )(places, core_t, grads, fresh)


def body(left, right, values, core, tile_slice, tile_fill):
    owners = lax.axis_size("own")
    groups = lax.axis_size("grp")
    tile_count, tile_rows, rank = left.shape
    per_device = core.shape[0]
    cap = 2 * tile_count // owners
    slots = owners * cap
    grp = lax.axis_index("grp")
    block = tile_slice // per_device
    owner = block % owners
    place = block // owners * per_device + tile_slice % per_device
    pos = jnp.arange(tile_count)
    earlier = (owner[:, None] == owner[None, :]) & (pos[None, :] < pos[:, None])
    slot_of_tile = owner * cap + jnp.sum(earlier.astype(jnp.int32), axis=1)
    match = slot_of_tile[None, :] == jnp.arange(slots)[:, None]
    live = jnp.any(match, axis=1)
    tile_of_slot = jnp.sum(jnp.where(match, pos[None, :], 0), axis=1)
    want = jnp.sum(jnp.where(match, place[None, :] + 1, 0), axis=1) - 1
    wide = jnp.pad(want.reshape(owners, 1, cap), ((0, 0), (0, 0), (0, LANES - cap)))
    table = swap(wide, groups, owners)[:, 0, :cap].reshape(groups, slots)

    def shifted(step):
        return (grp + step) % groups

    core_t = jnp.transpose(core, (1, 2, 0))
    local = table - grp * per_device
    mine = table[grp]
    order = [shifted(step) for step in range(groups)]
    found = fetch(core_t, jnp.concatenate([local[g] for g in order])[:, None])
    old, slices = deliver(jnp.transpose(found, (1, 0, 2)), groups, owners)
    tables = unpack(slices[slot_of_tile])

    projected = jnp.einsum("sea,sab->seb", left, tables, preferred_element_type=jnp.float32)
    predicted = jnp.sum(projected * right.astype(jnp.float32), axis=-1)
    live_rows = jnp.arange(tile_rows)[None, :] < tile_fill[:, None]
    residual = jnp.where(live_rows, predicted - values.astype(jnp.float32), 0.0)
    weighted = (residual[:, :, None] * left.astype(jnp.float32)).astype(jnp.bfloat16)
    grad = jnp.einsum("sea,seb->sab", weighted, right, preferred_element_type=jnp.float32).astype(jnp.bfloat16)
    send = jnp.where(live[:, None, None], pack(grad)[tile_of_slot], jnp.bfloat16(0))
    flat = collect(send, groups, owners)
    places = [mine]
    for step in range(1, groups):
        places.append(table[shifted(-step)])
    place_of = jnp.concatenate(places, axis=0)
    pick = (mine[:, None] == place_of[None, :]).astype(jnp.bfloat16)
    total = jnp.einsum("st,tab->sab", pick, flat, preferred_element_type=jnp.float32)
    fresh = (old.astype(jnp.float32) - total).astype(jnp.bfloat16)
    new_core_t, back = finish(
        core_t, jnp.transpose(flat, (1, 0, 2)), (place_of - grp * per_device)[:, None], fresh, owners
    )
    new_core = jnp.transpose(new_core_t, (2, 0, 1))
    new_left = jnp.einsum(
        "sea,sab->seb", left, unpack(back[slot_of_tile]), preferred_element_type=jnp.float32
    ).astype(jnp.bfloat16)
    return new_core, new_left


def solution(mesh):
    tiles = P(("grp", "own"), None, None)
    return jax.shard_map(
        body,
        mesh=mesh,
        in_specs=(tiles, tiles, P(("grp", "own"), None), tiles, P(("grp", "own")), P(("grp", "own"))),
        out_specs=(tiles, tiles),
        check_vma=False,
    )
```
